256 devices in a mesh: row: 8 (over y, core), col: 32 (over z, x).
Axes of the slice: x: 4, y: 4, z: 8, core: 2. Of those that a mesh axis runs over, the one named last changes fastest.
Arguments:
- ainv: bfloat16 [2, 32, 512, 8, 8, 512], P(None, 'col', None, None, 'row'), may hold values from -6 to 6
- panel: bfloat16 [2, 8, 8, 512, 512], P(None, None, 'row', 'col'), may hold values from -0.03125 to 0.03125
- pattern: int32 [2, 64], replicated, may hold values 0 or 1
- dinv: bfloat16 [2, 512, 512], replicated, may hold values from -6 to 6
Outputs:
- column_blocks: bfloat16 [2, 2, 32, 512, 512], P(None, None, 'col')
- diagonal: bfloat16 [2, 512, 512], replicated
The draws below stay inside these ranges and needn't reach their ends.
All inputs are finite; a program needn't handle non-finite values.
Results may differ from the reference program's by a relative error of at most 0.0034.
Values may be sent and summed in bfloat16 or wider, within the bound.
No kernel may reach another device: no remote copies, remote signals or barrier semaphores. Data moves between devices by JAX's collectives and lax.ppermute only.
A program may use at most 128 MiB of HBM per device.

```python
import jax
import jax.numpy as jnp
from jax import lax

B = 512
IBK = 2
S = 64
JBK = 8
N = 32768
N_ROW = 8
N_COL = 32


def set_ends(drawn, own_key, smallest, largest):
    longest = drawn.shape.index(max(drawn.shape))
    spots = []
    for shift in (0, 1):
        where = [jax.random.randint(jax.random.fold_in(own_key, axis), (), 0, length) for axis, length in enumerate(drawn.shape)]
        where[longest] = (where[longest] + shift) % drawn.shape[longest]
        spots.append(tuple(where))
    return drawn.at[spots[0]].set(smallest).at[spots[1]].set(largest)


def shard_levels(stream_key, shape, shards, least, top_value):
    loudness = 1.0
    for dim, shards_of in shards:
        draws = jax.random.uniform(jax.random.fold_in(jax.random.fold_in(stream_key, 6), dim), (shards_of,), jnp.float32, least / len(shards), top_value / len(shards))
        loudness = loudness * jnp.repeat(jnp.exp(draws), shape[dim] // shards_of).reshape((-1,) + (1,) * (len(shape) - 1 - dim))
    return loudness


def bell_draw(own_key, dims, deviation, reach, shards=(), dtype=jnp.bfloat16):
    array = deviation * jax.random.normal(own_key, dims, jnp.float32)
    if shards:
        array = array * shard_levels(own_key, dims, shards, -0.22, 0.18)
    return jnp.clip(array, -reach, reach).astype(dtype)


def setup_inputs(seed: int = 0) -> dict:
    keys = jax.random.split(jax.random.key(seed), 5)
    return {
        "ainv": bell_draw(keys[0], (IBK, N_COL, B, JBK, N_ROW, B), 1.0, 6.0, ((1, 32), (4, 8))),
        "panel": bell_draw(keys[1], (2, JBK, N_ROW, B, B), N ** -0.5, 0.03125, ((2, 8), (3, 32))),
        "pattern": set_ends((jax.random.randint(keys[2], (2, S), 0, 4) < 3).astype(jnp.int32), jax.random.fold_in(keys[2], 1), 0, 1),
        "dinv": bell_draw(keys[3], (2, B, B), 1.0, 6.0),
    }


def reference(ainv, panel, pattern, dinv):
    lower = panel.reshape(2, N, B)
    rowmask = jnp.repeat(pattern, B, axis=1)
    masked = jnp.where(rowmask[:, :, None] > 0, lower, jnp.zeros_like(lower))
    stacked = jnp.concatenate([masked[0], masked[1]], axis=1)
    blocks = ainv.reshape(S, B, N)

    def one_block(rows):
        return jnp.dot(rows, stacked, preferred_element_type=jnp.float32)

    product = lax.map(one_block, blocks)
    product = product.reshape(S, B, 2, B).transpose(2, 0, 1, 3).reshape(2, N, B)
    upper = -jnp.where(rowmask[:, :, None] > 0, product, jnp.zeros_like(product))
    rounded = upper.astype(jnp.bfloat16)
    column_blocks = rounded.reshape(2, IBK, N_COL, B, B)
    inner = jnp.einsum("kna,knb->kab", masked.astype(jnp.float32), rounded.astype(jnp.float32), precision=lax.Precision.HIGHEST)
    diagonal = (dinv.astype(jnp.float32) - inner).astype(jnp.bfloat16)
    return column_blocks, diagonal
```

```python
import jax
import jax.numpy as jnp
from jax import lax
from jax.sharding import PartitionSpec as P

BF16 = jnp.bfloat16
F32 = jnp.float32
CORES = 2


def row_pairs(y_size, shift):
    return [(y * CORES + core, (y + shift) % y_size * CORES + core) for y in range(y_size) for core in range(CORES)]


def core_pairs(y_size):
    return [(y * CORES + core, y * CORES + 1 - core) for y in range(y_size) for core in range(CORES)]


def y_groups(y_size):
    return [[y * CORES + core for y in range(y_size)] for core in range(CORES)]


def swap_cores(block, y_size):
    return lax.ppermute(block, "row", core_pairs(y_size))


def gather_y(own, y_at, y_size):
    out = jnp.zeros((y_size,) + own.shape, own.dtype)
    out = lax.dynamic_update_index_in_dim(out, own, y_at, 0)
    for shift in range(1, y_size):
        got = lax.ppermute(own, "row", row_pairs(y_size, shift))
        out = lax.dynamic_update_index_in_dim(out, got, (y_at - shift) % y_size, 0)
    return out.reshape((y_size * own.shape[0],) + own.shape[1:])


def scatter_sum_y(block, y_at, y_size):
    slabs = block.reshape((y_size, block.shape[0] // y_size) + block.shape[1:])
    total = lax.dynamic_index_in_dim(slabs, y_at, 0, keepdims=False)
    for shift in range(1, y_size):
        piece = lax.dynamic_index_in_dim(slabs, (y_at + shift) % y_size, 0, keepdims=False)
        total = total + lax.ppermute(piece, "row", row_pairs(y_size, shift))
    return total


def gather_panel(own):
    kk, jbk, part, width = own.shape
    return lax.all_gather(own, "col", axis=2, tiled=True).reshape(kk, -1, width)


def body(ainv, panel, pattern, dinv):
    row_count = lax.axis_size("row")
    col_count = lax.axis_size("col")
    row_at = lax.axis_index("row")
    col_at = lax.axis_index("col")
    y_size = row_count // CORES
    y_at = row_at // CORES
    core = row_at % CORES
    ibk, width, jbk = ainv.shape[0], ainv.shape[2], ainv.shape[3]
    kk = panel.shape[0]
    ratio = col_count // row_count
    holder = col_at % row_count
    quarter = col_at // row_count

    keep_cols = lax.dynamic_index_in_dim(pattern.reshape(kk, jbk, row_count), row_at, 2, keepdims=False)
    own = panel[:, :, 0]
    own = jnp.where(keep_cols[:, :, None, None] > 0, own, jnp.zeros_like(own))
    masked = gather_panel(own)

    inverse = ainv.reshape(ibk, width, jbk * width)
    mine = lax.dynamic_index_in_dim(inverse, core, 0, keepdims=False)
    theirs = lax.dynamic_index_in_dim(inverse, 1 - core, 0, keepdims=False)
    keep_rows = lax.dynamic_index_in_dim(pattern.reshape(kk, ibk, col_count), col_at, 2, keepdims=False)
    keep_rows = lax.dynamic_index_in_dim(keep_rows, core, 1, keepdims=False)

    blocks = masked.reshape(kk, ibk, ratio, width, width)
    blocks = lax.dynamic_index_in_dim(blocks, quarter, 2, keepdims=False)
    for_me = lax.dynamic_index_in_dim(blocks, core, 1, keepdims=False)
    for_sibling = lax.dynamic_index_in_dim(blocks, 1 - core, 1, keepdims=False)
    from_sibling = swap_cores(for_sibling, y_size)
    lower = jnp.where(holder % CORES == core, for_me, from_sibling)
    slab = width // y_size
    parts = lower.reshape(kk, width, y_size, slab).transpose(2, 0, 1, 3)
    parts = lax.all_to_all(parts, "row", 0, 0, axis_index_groups=y_groups(y_size))
    lower_part = lax.dynamic_index_in_dim(parts, holder // CORES, 0, keepdims=False)

    columns = []
    terms = []
    for k in range(kk):
        sent = swap_cores(jnp.dot(theirs, masked[k], preferred_element_type=F32), y_size)
        both = jnp.dot(mine, masked[k], preferred_element_type=F32) + sent
        total = scatter_sum_y(both, y_at, y_size)
        upper = -jnp.where(keep_rows[k] > 0, total, jnp.zeros_like(total))
        column = gather_y(upper.astype(BF16), y_at, y_size)
        other = swap_cores(column, y_size)
        columns.append(jnp.stack([jnp.where(core == 0, column, other), jnp.where(core == 0, other, column)]))
        term = lax.dot_general(lower_part[k], column, (((0,), (0,)), ((), ())), preferred_element_type=F32)
        half = term.reshape(CORES, slab // CORES, width)
        kept = lax.dynamic_index_in_dim(half, core, 0, keepdims=False)
        given = lax.dynamic_index_in_dim(half, 1 - core, 0, keepdims=False)
        terms.append(kept + swap_cores(given, y_size))
    column_blocks = jnp.stack(columns).reshape(kk, ibk, 1, width, width)

    rows = slab // CORES
    term = jnp.stack(terms)
    share = rows * width // col_count
    shares = term.reshape(kk, col_count, share // 128, 128).transpose(1, 0, 2, 3)
    summed = jnp.sum(lax.all_to_all(shares, "col", 0, 0), axis=0)
    base = lax.dynamic_slice_in_dim(dinv, row_at * rows, rows, 1)
    base = base.reshape(kk, col_count, share // 128, 128)
    base = lax.dynamic_index_in_dim(base, col_at, 1, keepdims=False)
    piece = (base.astype(F32) - summed).astype(BF16)
    pieces = jnp.broadcast_to(piece[None], (col_count,) + piece.shape)
    pieces = lax.all_to_all(pieces, "col", 0, 0)
    half = pieces.transpose(1, 0, 2, 3).reshape(kk, rows, width)
    other = swap_cores(half, y_size)
    pair = jnp.stack([jnp.where(core == 0, half, other), jnp.where(core == 0, other, half)], axis=1)
    pair = pair.reshape(kk, slab, width).transpose(1, 0, 2)
    diagonal = gather_y(pair, y_at, y_size).transpose(1, 0, 2)
    return (column_blocks, diagonal)


def solution(mesh):
    placed = (P(None, "col", None, None, "row", None), P(None, None, "row", "col", None), P(), P())
    return jax.shard_map(
        body,
        mesh=mesh,
        in_specs=placed,
        out_specs=(P(None, None, "col", None, None), P()),
        check_vma=False,
    )
```

```python
import jax
import jax.numpy as jnp
from jax import lax
from jax.experimental.layout import Layout, with_layout_constraint
from jax.sharding import PartitionSpec as P

BF16 = jnp.bfloat16
F32 = jnp.float32
CORES = 2
X_SIZE = 4


def row_pairs(y_size, shift):
    return [(y * CORES + core, (y + shift) % y_size * CORES + core) for y in range(y_size) for core in range(CORES)]


def core_pairs(y_size):
    return [(y * CORES + core, y * CORES + 1 - core) for y in range(y_size) for core in range(CORES)]


def y_groups(y_size):
    return [[y * CORES + core for y in range(y_size)] for core in range(CORES)]


def swap_cores(block, y_size):
    return lax.ppermute(block, "row", core_pairs(y_size))


def in_rows(block):
    return with_layout_constraint(block, Layout(tuple(range(block.ndim))))


def gather_y(own, y_at, y_size):
    kk, slab, width = own.shape
    out = jnp.zeros((kk, y_size * slab, width), own.dtype)

    def step(block, shift):
        return lax.ppermute(block, "row", row_pairs(y_size, shift))

    for shift, first, got in ring_gather(own, y_size, step):
        out = lax.dynamic_update_slice(out, got, (first, (y_at - shift) % y_size * slab, 0))
    return in_rows(out)


def scatter_sum_y(block, y_at, y_size):
    slabs = block.reshape((y_size, block.shape[0] // y_size) + block.shape[1:])
    half = slabs.shape[1] // 2

    def slab(shift):
        return lax.dynamic_index_in_dim(slabs, (y_at + shift) % y_size, 0, keepdims=False)

    far = slab(2)
    ahead = lax.ppermute(far[:half], "row", row_pairs(y_size, 1))
    back = lax.ppermute(far[half:], "row", row_pairs(y_size, -1))
    near = slab(1)
    near = jnp.concatenate([near[:half] + ahead, near[half:]])
    total = slab(0) + lax.ppermute(near, "row", row_pairs(y_size, 1))
    near = slab(-1)
    near = jnp.concatenate([near[:half], near[half:] + back])
    return total + lax.ppermute(near, "row", row_pairs(y_size, -1))


def col_pairs(x_size, z_size, x_shift, z_shift):
    return [
        (z * x_size + x, (z + z_shift) % z_size * x_size + (x + x_shift) % x_size)
        for z in range(z_size)
        for x in range(x_size)
    ]


def ring_gather(block, size, step):
    rows = block.shape[0]
    half = rows // 2
    ahead = back = block
    arrived = [(0, 0, block)]
    for hop in range(1, size // 2):
        ahead, back = step(ahead, 1), step(back, -1)
        arrived += [(hop, 0, ahead), (-hop, 0, back)]
    arrived += [(size // 2, 0, step(ahead[:half], 1)), (size // 2, half, step(back[half:], -1))]
    return arrived


def gather_panel(own):
    kk, jbk, part, width = own.shape
    x_size = X_SIZE
    z_size = lax.axis_size("col") // x_size
    z_at = lax.axis_index("col") // x_size
    x_at = lax.axis_index("col") % x_size

    def step_x(block, shift):
        return lax.ppermute(block, "col", col_pairs(x_size, z_size, shift, 0))

    def step_z(block, shift):
        return lax.ppermute(block, "col", col_pairs(x_size, z_size, 0, shift))

    def put_z(out, shift, got, first=0):
        return lax.dynamic_update_slice(out, jnp.expand_dims(got, 1), (first, (z_at - shift) % z_size) + (0,) * (out.ndim - 2))

    def put_x(out, shift, got, first=0):
        at = (first,) + (0,) * (out.ndim - 4) + ((x_at - shift) % x_size, 0, 0)
        return lax.dynamic_update_slice(out, jnp.expand_dims(got, -3), at)

    def both_ways(step, ahead, back):
        return step(ahead, 1), step(back, -1)

    zero, one = own[0], own[1]
    half = jbk // 2
    one_1 = both_ways(step_z, one, one)
    zero_x = put_x(jnp.zeros((jbk, x_size, part, width), own.dtype), 0, zero)
    for shift in (1, -1, 2):
        zero_x = put_x(zero_x, shift, step_x(zero, shift))
    one_2 = both_ways(step_z, *one_1)
    zero_x, one_2 = lax.optimization_barrier((zero_x, one_2))
    zero_1 = both_ways(step_z, zero_x, zero_x)
    one_3 = both_ways(step_z, *one_2)
    zero_1, one_3 = lax.optimization_barrier((zero_1, one_3))
    zero_2 = both_ways(step_z, *zero_1)
    one_4 = both_ways(step_z, one_3[0][:half], one_3[1][half:])
    one_z = put_z(jnp.zeros((jbk, z_size, part, width), own.dtype), 0, one)
    for hop, got in enumerate((one_1, one_2, one_3)):
        one_z = put_z(put_z(one_z, hop + 1, got[0]), -hop - 1, got[1])
    one_z = put_z(put_z(one_z, z_size // 2, one_4[0]), z_size // 2, one_4[1], half)
    far_1 = both_ways(step_x, one_z, one_z)
    zero_3 = both_ways(step_z, *zero_2)
    far_2 = both_ways(step_x, far_1[0][:half], far_1[1][half:])
    zero_4 = both_ways(step_z, zero_3[0][:half], zero_3[1][half:])
    zero_all = put_z(jnp.zeros((jbk, z_size, x_size, part, width), own.dtype), 0, zero_x)
    for hop, got in enumerate((zero_1, zero_2, zero_3)):
        zero_all = put_z(put_z(zero_all, hop + 1, got[0]), -hop - 1, got[1])
    zero_all = put_z(put_z(zero_all, z_size // 2, zero_4[0]), z_size // 2, zero_4[1], half)
    one_all = put_x(jnp.zeros((jbk, z_size, x_size, part, width), own.dtype), 0, one_z)
    one_all = put_x(put_x(one_all, 1, far_1[0]), -1, far_1[1])
    one_all = put_x(put_x(one_all, x_size // 2, far_2[0]), x_size // 2, far_2[1], half)
    return [zero_all.reshape(-1, width), one_all.reshape(-1, width)]


def body(ainv, panel, pattern, dinv):
    row_count = lax.axis_size("row")
    col_count = lax.axis_size("col")
    row_at = lax.axis_index("row")
    col_at = lax.axis_index("col")
    y_size = row_count // CORES
    y_at = row_at // CORES
    core = row_at % CORES
    ibk, width, jbk = ainv.shape[0], ainv.shape[2], ainv.shape[3]
    kk = panel.shape[0]
    ratio = col_count // row_count
    holder = col_at % row_count
    quarter = col_at // row_count

    keep_cols = lax.dynamic_index_in_dim(pattern.reshape(kk, jbk, row_count), row_at, 2, keepdims=False)
    own = panel[:, :, 0]
    own = jnp.where(keep_cols[:, :, None, None] > 0, own, jnp.zeros_like(own))
    masked = gather_panel(own)

    inverse = ainv.reshape(ibk, width, jbk, width)
    keep_rows = lax.dynamic_index_in_dim(pattern.reshape(kk, ibk, col_count), col_at, 2, keepdims=False)
    keep_rows = lax.dynamic_index_in_dim(keep_rows, core, 1, keepdims=False)

    def block_of(i):
        at = (i * ratio + quarter) * width
        return jnp.stack([lax.dynamic_slice_in_dim(one, at, width, 0) for one in masked])

    for_me = block_of(core)
    for_sibling = block_of(1 - core)
    from_sibling = swap_cores(for_sibling, y_size)
    lower = jnp.where(holder % CORES == core, for_me, from_sibling)
    slab = width // y_size
    lower = in_rows(lower)
    parts = in_rows(lower.reshape(kk, width, y_size, slab).transpose(2, 0, 1, 3))
    parts = in_rows(lax.all_to_all(parts, "row", 0, 0, axis_index_groups=y_groups(y_size)))
    lower_part = lax.dynamic_index_in_dim(parts, holder // CORES, 0, keepdims=False)

    uppers = []
    for k in range(kk):
        panels = masked[k].reshape(jbk, width, width)
        sums = in_rows(jnp.einsum("iajb,jbn->ian", inverse, panels, preferred_element_type=F32))
        sent = swap_cores(jnp.where(core == 0, sums[1], sums[0]), y_size)
        both = jnp.where(core == 0, sums[0], sums[1]) + sent
        total = scatter_sum_y(both, y_at, y_size)
        upper = -jnp.where(keep_rows[k] > 0, total, jnp.zeros_like(total))
        uppers.append(upper.astype(BF16))
    column = gather_y(in_rows(jnp.stack(uppers)), y_at, y_size)
    other = swap_cores(column, y_size)
    column_blocks = jnp.stack([jnp.where(core == 0, column, other), jnp.where(core == 0, other, column)], axis=1)
    column_blocks = column_blocks.reshape(kk, ibk, 1, width, width)
    term = lax.dot_general(lower_part, column, (((1,), (1,)), ((0,), (0,))), preferred_element_type=F32)
    term = in_rows(term)
    half = term.reshape(kk, CORES, slab // CORES, width)
    kept = lax.dynamic_index_in_dim(half, core, 1, keepdims=False)
    given = lax.dynamic_index_in_dim(half, 1 - core, 1, keepdims=False)
    term = kept + swap_cores(given, y_size)

    rows = slab // CORES
    share = rows * width // col_count
    shares = term.reshape(kk, col_count, share // 128, 128).transpose(1, 0, 2, 3)
    summed = jnp.sum(lax.all_to_all(shares, "col", 0, 0), axis=0)
    base = lax.dynamic_slice_in_dim(dinv, row_at * rows, rows, 1)
    base = base.reshape(kk, col_count, share // 128, 128)
    base = lax.dynamic_index_in_dim(base, col_at, 1, keepdims=False)
    piece = (base.astype(F32) - summed).astype(BF16)
    pieces = jnp.broadcast_to(piece[None], (col_count,) + piece.shape)
    pieces = lax.all_to_all(pieces, "col", 0, 0)
    half = pieces.transpose(1, 0, 2, 3).reshape(kk, rows, width)
    other = swap_cores(half, y_size)
    pair = jnp.concatenate([jnp.where(core == 0, half, other), jnp.where(core == 0, other, half)], axis=1)
    diagonal = gather_y(pair, y_at, y_size)
    return (column_blocks, diagonal)


def solution(mesh):
    placed = (P(None, "col", None, None, "row", None), P(None, None, "row", "col", None), P(), P())
    return jax.shard_map(
        body,
        mesh=mesh,
        in_specs=placed,
        out_specs=(P(None, None, "col", None, None), P()),
        check_vma=False,
    )
```

```python
import jax
import jax.numpy as jnp
from jax import lax
from jax.experimental.layout import Layout, with_layout_constraint
from jax.sharding import PartitionSpec as P

BF16 = jnp.bfloat16
F32 = jnp.float32
CORES = 2
X_SIZE = 4


def row_pairs(y_size, shift):
    return [(y * CORES + core, (y + shift) % y_size * CORES + core) for y in range(y_size) for core in range(CORES)]


def core_pairs(y_size):
    return [(y * CORES + core, y * CORES + 1 - core) for y in range(y_size) for core in range(CORES)]


def y_groups(y_size):
    return [[y * CORES + core for y in range(y_size)] for core in range(CORES)]


def swap_cores(block, y_size):
    return lax.ppermute(block, "row", core_pairs(y_size))


def in_rows(block):
    return with_layout_constraint(block, Layout(tuple(range(block.ndim))))


def gather_y(own, y_at, y_size):
    kk, slab, width = own.shape
    out = jnp.zeros((kk, y_size * slab, width), own.dtype)

    def step(block, shift):
        return lax.ppermute(block, "row", row_pairs(y_size, shift))

    for shift, first, got in ring_gather(own, y_size, step):
        out = lax.dynamic_update_slice(out, got, (first, (y_at - shift) % y_size * slab, 0))
    return in_rows(out)


def scatter_sum_y(block, y_at, y_size):
    slabs = block.reshape((y_size, block.shape[0] // y_size) + block.shape[1:])

    def slab(shift):
        return lax.dynamic_index_in_dim(slabs, (y_at + shift) % y_size, 0, keepdims=False)

    total = slab(0)
    for shift in (1, -1, 2):
        got = lax.ppermute(slab(shift).astype(BF16), "row", row_pairs(y_size, shift))
        total = total + got.astype(F32)
    return total


def col_pairs(x_size, z_size, x_shift, z_shift):
    return [
        (z * x_size + x, (z + z_shift) % z_size * x_size + (x + x_shift) % x_size)
        for z in range(z_size)
        for x in range(x_size)
    ]


def ring_gather(block, size, step):
    rows = block.shape[0]
    half = rows // 2
    ahead = back = block
    arrived = [(0, 0, block)]
    for hop in range(1, size // 2):
        ahead, back = step(ahead, 1), step(back, -1)
        arrived += [(hop, 0, ahead), (-hop, 0, back)]
    arrived += [(size // 2, 0, step(ahead[:half], 1)), (size // 2, half, step(back[half:], -1))]
    return arrived


def gather_panel(own, ainv):
    kk, jbk, part, width = own.shape
    x_size = X_SIZE
    z_size = lax.axis_size("col") // x_size
    z_at = lax.axis_index("col") // x_size
    x_at = lax.axis_index("col") % x_size

    def step_x(block, shift):
        return lax.ppermute(block, "col", col_pairs(x_size, z_size, shift, 0))

    def step_z(block, shift):
        return lax.ppermute(block, "col", col_pairs(x_size, z_size, 0, shift))

    def put_z(out, shift, got, first=0):
        return lax.dynamic_update_slice(out, jnp.expand_dims(got, 1), (first, (z_at - shift) % z_size) + (0,) * (out.ndim - 2))

    def put_x(out, shift, got, first=0):
        at = (first,) + (0,) * (out.ndim - 4) + ((x_at - shift) % x_size, 0, 0)
        return lax.dynamic_update_slice(out, jnp.expand_dims(got, -3), at)

    def both_ways(step, ahead, back):
        return step(ahead, 1), step(back, -1)

    zero, one = own[0], own[1]
    half = jbk // 2
    one_1 = both_ways(step_z, one, one)
    zero_x = put_x(jnp.zeros((jbk, x_size, part, width), own.dtype), 0, zero)
    for shift in (1, -1, 2):
        zero_x = put_x(zero_x, shift, step_x(zero, shift))
    one_2 = both_ways(step_z, *one_1)
    zero_x, one_2 = lax.optimization_barrier((zero_x, one_2))
    zero_1 = both_ways(step_z, zero_x, zero_x)
    one_3 = both_ways(step_z, *one_2)
    zero_1, one_3 = lax.optimization_barrier((zero_1, one_3))
    zero_2 = both_ways(step_z, *zero_1)
    one_4 = both_ways(step_z, one_3[0][:half], one_3[1][half:])
    one_z = put_z(jnp.zeros((jbk, z_size, part, width), own.dtype), 0, one)
    for hop, got in enumerate((one_1, one_2, one_3)):
        one_z = put_z(put_z(one_z, hop + 1, got[0]), -hop - 1, got[1])
    one_z = put_z(put_z(one_z, z_size // 2, one_4[0]), z_size // 2, one_4[1], half)
    far_1 = both_ways(step_x, one_z, one_z)
    zero_3 = both_ways(step_z, *zero_2)
    ainv, zero_3 = lax.optimization_barrier((ainv, zero_3))
    far_2 = both_ways(step_x, far_1[0][:half], far_1[1][half:])
    zero_4 = both_ways(step_z, zero_3[0][:half], zero_3[1][half:])
    zero_all = put_z(jnp.zeros((jbk, z_size, x_size, part, width), own.dtype), 0, zero_x)
    for hop, got in enumerate((zero_1, zero_2, zero_3)):
        zero_all = put_z(put_z(zero_all, hop + 1, got[0]), -hop - 1, got[1])
    zero_all = put_z(put_z(zero_all, z_size // 2, zero_4[0]), z_size // 2, zero_4[1], half)
    one_all = put_x(jnp.zeros((jbk, z_size, x_size, part, width), own.dtype), 0, one_z)
    one_all = put_x(put_x(one_all, 1, far_1[0]), -1, far_1[1])
    one_all = put_x(put_x(one_all, x_size // 2, far_2[0]), x_size // 2, far_2[1], half)
    return [zero_all.reshape(-1, width), one_all.reshape(-1, width)], ainv


def body(ainv, panel, pattern, dinv):
    row_count = lax.axis_size("row")
    col_count = lax.axis_size("col")
    row_at = lax.axis_index("row")
    col_at = lax.axis_index("col")
    y_size = row_count // CORES
    y_at = row_at // CORES
    core = row_at % CORES
    ibk, width, jbk = ainv.shape[0], ainv.shape[2], ainv.shape[3]
    kk = panel.shape[0]
    ratio = col_count // row_count
    holder = col_at % row_count
    quarter = col_at // row_count

    keep_cols = lax.dynamic_index_in_dim(pattern.reshape(kk, jbk, row_count), row_at, 2, keepdims=False)
    own = panel[:, :, 0]
    own = jnp.where(keep_cols[:, :, None, None] > 0, own, jnp.zeros_like(own))
    masked, ainv = gather_panel(own, ainv)

    inverse = ainv.reshape(ibk, width, jbk, width)
    keep_rows = lax.dynamic_index_in_dim(pattern.reshape(kk, ibk, col_count), col_at, 2, keepdims=False)
    keep_rows = lax.dynamic_index_in_dim(keep_rows, core, 1, keepdims=False)

    def block_of(i):
        at = (i * ratio + quarter) * width
        return jnp.stack([lax.dynamic_slice_in_dim(one, at, width, 0) for one in masked])

    for_me = block_of(core)
    for_sibling = block_of(1 - core)
    from_sibling = swap_cores(for_sibling, y_size)
    lower = jnp.where(holder % CORES == core, for_me, from_sibling)
    slab = width // y_size
    lower = in_rows(lower)
    parts = in_rows(jnp.stack([lower[:, :, at * slab : (at + 1) * slab] for at in range(y_size)]))
    parts = in_rows(lax.all_to_all(parts, "row", 0, 0, axis_index_groups=y_groups(y_size)))
    lower_part = lax.dynamic_index_in_dim(parts, holder // CORES, 0, keepdims=False)

    uppers = []
    for k in range(kk):
        panels = masked[k].reshape(jbk, width, width)
        sums = in_rows(jnp.einsum("iajb,jbn->ian", inverse, panels, preferred_element_type=F32))
        sent = swap_cores(jnp.where(core == 0, sums[1], sums[0]), y_size)
        both = jnp.where(core == 0, sums[0], sums[1]) + sent
        total = scatter_sum_y(both, y_at, y_size)
        upper = -jnp.where(keep_rows[k] > 0, total, jnp.zeros_like(total))
        uppers.append(upper.astype(BF16))
    column = gather_y(in_rows(jnp.stack(uppers)), y_at, y_size)
    other = swap_cores(column, y_size)
    column_blocks = jnp.stack([jnp.where(core == 0, column, other), jnp.where(core == 0, other, column)], axis=1)
    column_blocks = column_blocks.reshape(kk, ibk, 1, width, width)
    term = lax.dot_general(lower_part, column, (((1,), (1,)), ((0,), (0,))), preferred_element_type=F32)
    term = in_rows(term)
    half = term.reshape(kk, CORES, slab // CORES, width)
    kept = lax.dynamic_index_in_dim(half, core, 1, keepdims=False)
    given = lax.dynamic_index_in_dim(half, 1 - core, 1, keepdims=False)
    term = kept + swap_cores(given, y_size)

    rows = slab // CORES
    share = rows * width // col_count
    shares = term.reshape(kk, col_count, share // 128, 128).transpose(1, 0, 2, 3)
    summed = jnp.sum(lax.all_to_all(shares, "col", 0, 0), axis=0)
    base = lax.dynamic_slice_in_dim(dinv, row_at * rows, rows, 1)
    base = base.reshape(kk, col_count, share // 128, 128)
    base = lax.dynamic_index_in_dim(base, col_at, 1, keepdims=False)
    piece = (base.astype(F32) - summed).astype(BF16)
    pieces = jnp.broadcast_to(piece[None], (col_count,) + piece.shape)
    pieces = lax.all_to_all(pieces, "col", 0, 0)
    half = pieces.transpose(1, 0, 2, 3).reshape(kk, rows, width)
    other = swap_cores(half, y_size)
    pair = jnp.concatenate([jnp.where(core == 0, half, other), jnp.where(core == 0, other, half)], axis=1)
    diagonal = gather_y(pair, y_at, y_size)
    return (column_blocks, diagonal)


def solution(mesh):
    placed = (P(None, "col", None, None, "row", None), P(None, None, "row", "col", None), P(), P())
    return jax.shard_map(
        body,
        mesh=mesh,
        in_specs=placed,
        out_specs=(P(None, None, "col", None, None), P()),
        check_vma=False,
    )
```

```python
import jax
import jax.numpy as jnp
from jax import lax
from jax.experimental.layout import Layout, with_layout_constraint
from jax.sharding import PartitionSpec as P

BF16 = jnp.bfloat16
F32 = jnp.float32
CORES = 2
X_SIZE = 4


def row_pairs(y_size, shift):
    return [(y * CORES + core, (y + shift) % y_size * CORES + core) for y in range(y_size) for core in range(CORES)]


def core_pairs(y_size):
    return [(y * CORES + core, y * CORES + 1 - core) for y in range(y_size) for core in range(CORES)]


def y_groups(y_size):
    return [[y * CORES + core for y in range(y_size)] for core in range(CORES)]


def swap_cores(block, y_size):
    return lax.ppermute(block, "row", core_pairs(y_size))


def in_rows(block):
    return with_layout_constraint(block, Layout(tuple(range(block.ndim))))


def gather_y(own, y_at, y_size):
    kk, slab, width = own.shape
    out = jnp.zeros((kk, y_size * slab, width), own.dtype)

    def step(block, shift):
        return lax.ppermute(block, "row", row_pairs(y_size, shift))

    for shift, first, got in ring_gather(own, y_size, step):
        out = lax.dynamic_update_slice(out, got, (first, (y_at - shift) % y_size * slab, 0))
    return in_rows(out)


def scatter_sum_y(block, y_at, y_size):
    slabs = block.reshape((y_size, block.shape[0] // y_size) + block.shape[1:])
    half = slabs.shape[1] // 2

    def slab(shift):
        return lax.dynamic_index_in_dim(slabs, (y_at + shift) % y_size, 0, keepdims=False)

    far = slab(2)
    ahead = lax.ppermute(far[:half], "row", row_pairs(y_size, 1))
    back = lax.ppermute(far[half:], "row", row_pairs(y_size, -1))
    near = slab(1)
    near = jnp.concatenate([near[:half] + ahead, near[half:]])
    total = slab(0) + lax.ppermute(near, "row", row_pairs(y_size, 1))
    near = slab(-1)
    near = jnp.concatenate([near[:half], near[half:] + back])
    return total + lax.ppermute(near, "row", row_pairs(y_size, -1))


def col_pairs(x_size, z_size, x_shift, z_shift):
    return [
        (z * x_size + x, (z + z_shift) % z_size * x_size + (x + x_shift) % x_size)
        for z in range(z_size)
        for x in range(x_size)
    ]


def ring_gather(block, size, step):
    rows = block.shape[0]
    half = rows // 2
    ahead = back = block
    arrived = [(0, 0, block)]
    for hop in range(1, size // 2):
        ahead, back = step(ahead, 1), step(back, -1)
        arrived += [(hop, 0, ahead), (-hop, 0, back)]
    arrived += [(size // 2, 0, step(ahead[:half], 1)), (size // 2, half, step(back[half:], -1))]
    return arrived


def gather_panel(own, ainv):
    kk, jbk, part, width = own.shape
    x_size = X_SIZE
    z_size = lax.axis_size("col") // x_size
    z_at = lax.axis_index("col") // x_size
    x_at = lax.axis_index("col") % x_size

    def step_x(block, shift):
        return lax.ppermute(block, "col", col_pairs(x_size, z_size, shift, 0))

    def step_z(block, shift):
        return lax.ppermute(block, "col", col_pairs(x_size, z_size, 0, shift))

    def put_z(out, shift, got, first=0):
        return lax.dynamic_update_slice(out, jnp.expand_dims(got, 1), (first, (z_at - shift) % z_size) + (0,) * (out.ndim - 2))

    def put_x(out, shift, got, first=0):
        at = (first,) + (0,) * (out.ndim - 4) + ((x_at - shift) % x_size, 0, 0)
        return lax.dynamic_update_slice(out, jnp.expand_dims(got, -3), at)

    def both_ways(step, ahead, back):
        return step(ahead, 1), step(back, -1)

    zero, one = own[0], own[1]
    half = jbk // 2
    one_1 = both_ways(step_z, one, one)
    zero_x = put_x(jnp.zeros((jbk, x_size, part, width), own.dtype), 0, zero)
    for shift in (1, -1, 2):
        zero_x = put_x(zero_x, shift, step_x(zero, shift))
    one_2 = both_ways(step_z, *one_1)
    zero_x, one_2 = lax.optimization_barrier((zero_x, one_2))
    zero_1 = both_ways(step_z, zero_x, zero_x)
    one_3 = both_ways(step_z, *one_2)
    zero_1, one_3 = lax.optimization_barrier((zero_1, one_3))
    zero_2 = both_ways(step_z, *zero_1)
    one_4 = both_ways(step_z, one_3[0][:half], one_3[1][half:])
    one_z = put_z(jnp.zeros((jbk, z_size, part, width), own.dtype), 0, one)
    for hop, got in enumerate((one_1, one_2, one_3)):
        one_z = put_z(put_z(one_z, hop + 1, got[0]), -hop - 1, got[1])
    one_z = put_z(put_z(one_z, z_size // 2, one_4[0]), z_size // 2, one_4[1], half)
    far_1 = both_ways(step_x, one_z, one_z)
    zero_3 = both_ways(step_z, *zero_2)
    ainv, zero_3 = lax.optimization_barrier((ainv, zero_3))
    far_2 = both_ways(step_x, far_1[0][:half], far_1[1][half:])
    zero_4 = both_ways(step_z, zero_3[0][:half], zero_3[1][half:])
    zero_all = put_z(jnp.zeros((jbk, z_size, x_size, part, width), own.dtype), 0, zero_x)
    for hop, got in enumerate((zero_1, zero_2, zero_3)):
        zero_all = put_z(put_z(zero_all, hop + 1, got[0]), -hop - 1, got[1])
    zero_all = put_z(put_z(zero_all, z_size // 2, zero_4[0]), z_size // 2, zero_4[1], half)
    one_all = put_x(jnp.zeros((jbk, z_size, x_size, part, width), own.dtype), 0, one_z)
    one_all = put_x(put_x(one_all, 1, far_1[0]), -1, far_1[1])
    one_all = put_x(put_x(one_all, x_size // 2, far_2[0]), x_size // 2, far_2[1], half)
    return [zero_all.reshape(-1, width), one_all.reshape(-1, width)], ainv


def body(ainv, panel, pattern, dinv):
    row_count = lax.axis_size("row")
    col_count = lax.axis_size("col")
    row_at = lax.axis_index("row")
    col_at = lax.axis_index("col")
    y_size = row_count // CORES
    y_at = row_at // CORES
    core = row_at % CORES
    ibk, width, jbk = ainv.shape[0], ainv.shape[2], ainv.shape[3]
    kk = panel.shape[0]
    ratio = col_count // row_count
    holder = col_at % row_count
    quarter = col_at // row_count

    keep_cols = lax.dynamic_index_in_dim(pattern.reshape(kk, jbk, row_count), row_at, 2, keepdims=False)
    own = panel[:, :, 0]
    own = jnp.where(keep_cols[:, :, None, None] > 0, own, jnp.zeros_like(own))
    masked, ainv = gather_panel(own, ainv)

    inverse = ainv.reshape(ibk, width, jbk, width)
    keep_rows = lax.dynamic_index_in_dim(pattern.reshape(kk, ibk, col_count), col_at, 2, keepdims=False)
    keep_rows = lax.dynamic_index_in_dim(keep_rows, core, 1, keepdims=False)

    def block_of(i):
        at = (i * ratio + quarter) * width
        return jnp.stack([lax.dynamic_slice_in_dim(one, at, width, 0) for one in masked])

    for_me = block_of(core)
    for_sibling = block_of(1 - core)
    from_sibling = swap_cores(for_sibling, y_size)
    lower = jnp.where(holder % CORES == core, for_me, from_sibling)
    slab = width // y_size
    lower = in_rows(lower)
    parts = in_rows(jnp.stack([lower[:, :, at * slab : (at + 1) * slab] for at in range(y_size)]))
    parts = in_rows(lax.all_to_all(parts, "row", 0, 0, axis_index_groups=y_groups(y_size)))
    lower_part = lax.dynamic_index_in_dim(parts, holder // CORES, 0, keepdims=False)

    uppers = []
    for k in range(kk):
        panels = masked[k].reshape(jbk, width, width)
        sums = in_rows(jnp.einsum("iajb,jbn->ian", inverse, panels, preferred_element_type=F32))
        sent = swap_cores(jnp.where(core == 0, sums[1], sums[0]), y_size)
        both = jnp.where(core == 0, sums[0], sums[1]) + sent
        total = scatter_sum_y(both, y_at, y_size)
        upper = -jnp.where(keep_rows[k] > 0, total, jnp.zeros_like(total))
        uppers.append(upper.astype(BF16))
    column = gather_y(in_rows(jnp.stack(uppers)), y_at, y_size)
    other = swap_cores(column, y_size)
    column_blocks = jnp.stack([jnp.where(core == 0, column, other), jnp.where(core == 0, other, column)], axis=1)
    column_blocks = column_blocks.reshape(kk, ibk, 1, width, width)
    term = lax.dot_general(lower_part, column, (((1,), (1,)), ((0,), (0,))), preferred_element_type=F32)
    term = in_rows(term)
    half = term.reshape(kk, CORES, slab // CORES, width)
    kept = lax.dynamic_index_in_dim(half, core, 1, keepdims=False)
    given = lax.dynamic_index_in_dim(half, 1 - core, 1, keepdims=False)
    term = kept + swap_cores(given, y_size)

    rows = slab // CORES
    share = rows * width // col_count
    shares = term.reshape(kk, col_count, share // 128, 128).transpose(1, 0, 2, 3)
    summed = jnp.sum(lax.all_to_all(shares, "col", 0, 0), axis=0)
    base = lax.dynamic_slice_in_dim(dinv, row_at * rows, rows, 1)
    base = base.reshape(kk, col_count, share // 128, 128)
    base = lax.dynamic_index_in_dim(base, col_at, 1, keepdims=False)
    piece = (base.astype(F32) - summed).astype(BF16)
    pieces = jnp.broadcast_to(piece[None], (col_count,) + piece.shape)
    pieces = lax.all_to_all(pieces, "col", 0, 0)
    half = pieces.transpose(1, 0, 2, 3).reshape(kk, rows, width)
    other = swap_cores(half, y_size)
    pair = jnp.concatenate([jnp.where(core == 0, half, other), jnp.where(core == 0, other, half)], axis=1)
    diagonal = gather_y(pair, y_at, y_size)
    return (column_blocks, diagonal)


def solution(mesh):
    placed = (P(None, "col", None, None, "row", None), P(None, None, "row", "col", None), P(), P())
    return jax.shard_map(
        body,
        mesh=mesh,
        in_specs=placed,
        out_specs=(P(None, None, "col", None, None), P()),
        check_vma=False,
    )
```
